32 devices in a mesh: row: 4 (over x, core), col: 8 (over z, y).
Axes of the slice: x: 2, y: 2, z: 4, core: 2. Of those that a mesh axis runs over, the one named last changes fastest.
Arguments:
- vectors: bfloat16 [16, 49152], P(None, ('row', 'col')), may hold values from -6 to 6
- tiles: bfloat16 [4096, 128, 128], P(('row', 'col')), may hold values from -0.046875 to 0.046875
- tile_rows: int32 [4096], P(('row', 'col')), may hold values from 0 to 95
- tile_cols: int32 [4096], P(('row', 'col')), may hold values from 0 to 95
- tile_count: int32 [32], P(('row', 'col')), may hold values from 32 to 128, as said below
Outputs:
- applied: float32 [16, 49152], P(None, ('row', 'col'))
The draws below stay inside these ranges and needn't reach their ends.
Inputs may be any that keep to these rules, and one draw needn't show every extreme that they name: `tile_count`: each device has between 32 and 128 live slots; some device fills all 128.
All inputs are finite; a program needn't handle non-finite values.
Results may differ from the reference program's by a relative error of at most 0.0003.
Values may be sent and summed in bfloat16 or wider, within the bound.
A program may use at most 64 MiB of HBM per device.

```python
import jax
import jax.numpy as jnp
from jax import lax

NVEC = 16
TILE = 128
TS = 96
TPD = 128
GROUPS = 32
SLOTS = 4096
NV = 49152
N_ROW = 4
N_COL = 8


def draw_tile_count(key, part):
    count_key, pick_key = jax.random.split(jax.random.fold_in(key, 17))
    lowered = TPD - jax.random.randint(count_key, (GROUPS,), 0, 3 * TPD // 4 + 1)
    fullest = jax.random.randint(pick_key, (), 0, GROUPS)
    return jnp.where(jnp.arange(GROUPS) == fullest, TPD, lowered).astype(jnp.int32)


def with_ends(values, stream_key, smallest, top_value):
    dims = values.shape
    place = [jax.random.randint(jax.random.fold_in(stream_key, axis), (), 0, dims[axis]) for axis in range(len(dims))]
    values = values.at[tuple(place)].set(smallest)
    longest = dims.index(max(dims))
    place[longest] = (place[longest] + 1) % dims[longest]
    return values.at[tuple(place)].set(top_value)


def block_levels(key, shape, shards, least, high):
    def one(dim, blocks):
        draws = jax.random.uniform(jax.random.fold_in(jax.random.fold_in(key, 6), dim), (blocks,), jnp.float32, least / len(shards), high / len(shards))
        return jnp.repeat(jnp.exp(draws), shape[dim] // blocks).reshape((-1,) + (1,) * (len(shape) - dim - 1))

    loudness = one(*shards[0])
    for cut in shards[1:]:
        loudness = loudness * one(*cut)
    return loudness


def bell_draw(rng, extent, width, bound, cuts=(), kind=jnp.bfloat16):
    array = jax.random.normal(rng, extent, jnp.float32) * width
    if len(cuts) > 0:
        array = block_levels(rng, extent, cuts, -0.22, 0.18) * array
    return jnp.clip(array, min=-bound, max=bound).astype(kind)


def setup_inputs(seed: int = 0) -> dict:
    streams_of = jax.random.split(jax.random.key(seed), 6)
    vectors = bell_draw(streams_of[0], (NVEC, NV), 1.0, 6.0, ((1, 32),))
    tiles = bell_draw(streams_of[1], (SLOTS, TILE, TILE), (TILE * TPD) ** -0.5, 0.046875, ((0, 32),))
    tile_rows = with_ends(jax.random.randint(streams_of[2], (SLOTS,), 0, TS), jax.random.fold_in(streams_of[2], 1), 0, TS - 1).astype(jnp.int32)
    tile_cols = with_ends(jax.random.randint(streams_of[3], (SLOTS,), 0, TS), jax.random.fold_in(streams_of[3], 1), 0, TS - 1).astype(jnp.int32)
    tile_count = draw_tile_count(jax.random.fold_in(streams_of[5], 71), 0)
    return dict(vectors=vectors, tiles=tiles, tile_rows=tile_rows, tile_cols=tile_cols, tile_count=tile_count)


def reference(vectors, tiles, tile_rows, tile_cols, tile_count):
    groups = N_ROW * N_COL
    xblocks = jnp.transpose(vectors.reshape(NVEC, N_ROW * TS, TILE), (1, 0, 2)).astype(jnp.float32)
    tile_sets = tiles.reshape(groups, TPD, TILE, TILE)
    row_sets = tile_rows.reshape(groups, TPD)
    col_sets = tile_cols.reshape(groups, TPD)

    def add_group(accum_rows, entries):
        group_id, tile_set, row_tiles, col_tiles, live_count = entries
        row_seg = group_id // N_COL
        col_seg = (group_id % N_COL) % N_ROW
        glob_rows = (row_seg * TS + row_tiles).astype(jnp.int32)
        glob_cols = (col_seg * TS + col_tiles).astype(jnp.int32)
        live_slots = jnp.arange(TPD, dtype=jnp.int32) < live_count
        mirrored = live_slots & (glob_rows != glob_cols)
        tile_values = tile_set.astype(jnp.float32)
        col_vectors = jnp.take(xblocks, glob_cols, axis=0)
        row_vectors = jnp.take(xblocks, glob_rows, axis=0)
        plain_terms = jnp.einsum("kvj,kij->kvi", col_vectors, tile_values)
        mirror_terms = jnp.einsum("kvi,kij->kvj", row_vectors, tile_values)
        plain_terms = jnp.where(live_slots[:, None, None], plain_terms, 0.0)
        mirror_terms = jnp.where(mirrored[:, None, None], mirror_terms, 0.0)
        accum_rows = accum_rows.at[glob_rows].add(plain_terms).at[glob_cols].add(mirror_terms)
        return accum_rows, None

    start = jnp.zeros((N_ROW * TS, NVEC, TILE), jnp.float32)
    group_ids = jnp.arange(groups, dtype=jnp.int32)
    accum_rows, _ = lax.scan(add_group, start, (group_ids, tile_sets, row_sets, col_sets, tile_count))
    return jnp.transpose(accum_rows, (1, 0, 2)).reshape(NVEC, N_ROW * TS * TILE)
```

```python
import functools

import jax
import jax.numpy as jnp
from jax import lax
from jax.experimental import pallas as pl
from jax.experimental.pallas import tpu as pltpu
from jax.sharding import PartitionSpec as P

MESH = pl.DeviceIdType.MESH
VMEM_BYTES = 32 * 1024 * 1024


def remote(src, dst, send_sem, recv_sem, row, col):
    return pltpu.make_async_remote_copy(
        src_ref=src,
        dst_ref=dst,
        send_sem=send_sem,
        recv_sem=recv_sem,
        device_id=(row, col),
        device_id_type=MESH,
    )


def greet(row, col):
    pl.semaphore_signal(
        pltpu.get_barrier_semaphore(), inc=1, device_id=(row, col), device_id_type=MESH
    )


def gather_kernel(rows, cols, width, x_ref, own, mir, line_send, mate_send, own_recv, mir_send, mir_recv):
    r, c = lax.axis_index("row"), lax.axis_index("col")
    half, row_half = cols // 2, rows // 2
    hi, lo = c // 2, c % 2
    mate = c + 1 - 2 * lo
    row_lo, row_hi = r % 2, r // 2
    row_mate = r + 1 - 2 * row_lo
    src = c % rows
    src_lo, src_hi = src % 2, src // 2
    size = own.shape[0] // cols
    is_src = r == src
    is_relay = (row_lo == src_lo) & (row_hi != src_hi)

    greet(r, mate)
    for d in range(1, half):
        greet(r, lax.rem(hi + half - d, half) * 2 + lo)

    @pl.when(jnp.logical_not(is_src))
    def _():
        from_src = (row_lo == src_lo) | (row_hi == src_hi)
        greet(jnp.where(from_src, src, row_mate), c)

    for t in range(size):
        own[c * size + t] = x_ref[:, t * width:(t + 1) * width]
    out_count = jnp.where(is_src, row_half, jnp.where(is_relay, 1, 0))
    pl.semaphore_wait(pltpu.get_barrier_semaphore(), half + out_count)

    def part(ref, index):
        return ref.at[pl.ds(index * size, size)]

    def to_line(d):
        there = lax.rem(hi + d, half) * 2 + lo
        return remote(part(own, c), part(own, c), line_send.at[d - 1], own_recv.at[c], r, there)

    def to_mate(index, n):
        return remote(part(own, index), part(own, index), mate_send.at[n], own_recv.at[index], r, mate)

    def arrived(index):
        remote(part(own, index), part(own, index), mate_send.at[0], own_recv.at[index], r, mate).wait_recv()

    def mirror_sends(index, n):
        copies = [remote(part(own, index), part(mir, index), mir_send.at[n, 0], mir_recv.at[index], row_mate, c)]
        for d in range(1, row_half):
            there = lax.rem(row_hi + d, row_half) * 2 + row_lo
            copies.append(
                remote(part(own, index), part(mir, index), mir_send.at[n, d], mir_recv.at[index], there, c)
            )
        return copies

    def relay(index, n):
        return remote(part(mir, index), part(mir, index), mir_send.at[n, 0], mir_recv.at[index], row_mate, c)

    order = [c]
    for d in range(1, half):
        order.append(lax.rem(hi + half - d, half) * 2 + lo)
    order.append(mate)
    for d in range(1, half):
        order.append(lax.rem(hi + half - d, half) * 2 + 1 - lo)

    for d in range(1, half):
        to_line(d).start()
    for n in range(cols):
        index = order[n]
        if n:
            arrived(index)
        if n < half:
            to_mate(index, n).start()

        @pl.when(is_src)
        def _(index=index, n=n):
            for copy in mirror_sends(index, n):
                copy.start()
            for t in range(size):
                mir[index * size + t] = own[index * size + t]

    @pl.when(jnp.logical_not(is_src))
    def _():
        for n in range(cols):
            index = order[n]
            relay(index, n).wait_recv()

            @pl.when(is_relay)
            def _(index=index, n=n):
                relay(index, n).start()

    for d in range(1, half):
        to_line(d).wait_send()
    for n in range(half):
        to_mate(order[n], n).wait_send()

    @pl.when(is_src)
    def _():
        for n in range(cols):
            for copy in mirror_sends(order[n], n):
                copy.wait_send()

    @pl.when(is_relay)
    def _():
        for n in range(cols):
            relay(order[n], n).wait_send()


def gather(vectors, rows, cols, width):
    vec_count, length = vectors.shape
    total = cols * (length // width)
    out = jax.ShapeDtypeStruct((total, vec_count, width), vectors.dtype)
    return pl.pallas_call(
        functools.partial(gather_kernel, rows, cols, width),
        out_shape=(out, out),
        in_specs=[pl.BlockSpec(memory_space=pltpu.VMEM)],
        out_specs=(pl.BlockSpec(memory_space=pltpu.VMEM),) * 2,
        scratch_shapes=[
            pltpu.SemaphoreType.DMA((cols // 2,)),
            pltpu.SemaphoreType.DMA((cols // 2,)),
            pltpu.SemaphoreType.DMA((cols,)),
            pltpu.SemaphoreType.DMA((cols, rows // 2)),
            pltpu.SemaphoreType.DMA((cols,)),
        ],
        compiler_params=pltpu.CompilerParams(
            collective_id=0, has_side_effects=True, vmem_limit_bytes=VMEM_BYTES
        ),
        name="gather_segments",
    )(vectors)


def tiles_kernel(block, group, rows_ref, cols_ref, info_ref, own, mir, tiles, plain, mirror):
    step = pl.program_id(0)
    spare = plain.shape[0] - 1

    @pl.when(step == 0)
    def _():
        plain[...] = jnp.zeros_like(plain)
        mirror[...] = jnp.zeros_like(mirror)

    count, off_diagonal = info_ref[0], info_ref[1]

    def body(g, carry):
        work = []
        for u in range(group):
            k = g * group + u
            slot = step * block + k
            row, col = rows_ref[slot], cols_ref[slot]
            live = slot < count
            both = live & ((off_diagonal != 0) | (row != col))
            tile = tiles[k]
            first = lax.dot_general(
                mir[col], tile, (((1,), (1,)), ((), ())), preferred_element_type=jnp.float32
            )
            second = lax.dot_general(
                own[row], tile, (((1,), (0,)), ((), ())), preferred_element_type=jnp.float32
            )
            work.append((jnp.where(live, row, spare), first, jnp.where(both, col, spare), second))
        for row, first, col, second in work:
            plain[row] += first
            mirror[col] += second
        return carry

    @pl.when(step * block < count)
    def _():
        lax.fori_loop(0, block // group, body, 0)


def apply_tiles(tile_rows, tile_cols, info, own, mir, tiles):
    slots, width = tiles.shape[0], tiles.shape[1]
    block = 16 if slots % 16 == 0 else slots
    group = 8 if block % 8 == 0 else 1
    total, vec_count = own.shape[0], own.shape[1]
    out = jax.ShapeDtypeStruct((total + 1, vec_count, width), jnp.float32)
    whole = pl.BlockSpec((total, vec_count, width), lambda i, *_: (0, 0, 0))
    summed = pl.BlockSpec((total + 1, vec_count, width), lambda i, *_: (0, 0, 0))
    return pl.pallas_call(
        functools.partial(tiles_kernel, block, group),
        out_shape=(out, out),
        grid_spec=pltpu.PrefetchScalarGridSpec(
            num_scalar_prefetch=3,
            grid=(slots // block,),
            in_specs=[whole, whole, pl.BlockSpec((block, width, width), lambda i, *_: (i, 0, 0))],
            out_specs=(summed, summed),
        ),
        compiler_params=pltpu.CompilerParams(
            dimension_semantics=("arbitrary",), vmem_limit_bytes=VMEM_BYTES
        ),
        name="apply_tiles",
    )(tile_rows, tile_cols, info, own, mir, tiles)


def reduce_kernel(
    rows, cols, width, plain, mirror, out,
    y_in, y_sum, z_in, a_in, a_sum, b_in, b_sum, m_in,
    y_send, y_recv, z_send, z_recv, a_send, a_recv, b_send, b_recv, m_send, m_recv,
):
    r, c = lax.axis_index("row"), lax.axis_index("col")
    half, row_half = cols // 2, rows // 2
    hi, lo = c // 2, c % 2
    mate = c + 1 - 2 * lo
    row_lo, row_hi = r % 2, r // 2
    row_mate = r + 1 - 2 * row_lo
    share = cols // rows
    target = c % rows
    turn = c // rows
    size = y_in.shape[1]
    owns = target == r

    def is_self(j):
        return owns & (share * r + j == c)

    greet(r, mate)
    for d in range(1, half):
        greet(r, lax.rem(hi + half - d, half) * 2 + lo)
    greet(row_mate, c)
    for d in range(1, row_half):
        greet(lax.rem(row_hi + row_half - d, row_half) * 2 + row_lo, c)
    for i in range(share):
        @pl.when(jnp.logical_not((c // share == r) & (r + rows * i == c)))
        def _(i=i):
            greet(c // share, r + rows * i)
    own_piece = (c // share == r) & owns
    pl.semaphore_wait(
        pltpu.get_barrier_semaphore(), half + row_half + share - jnp.where(own_piece, 1, 0)
    )

    def part(ref, index, count=1):
        return ref.at[pl.ds(index * size, count * size)]

    def a_copy(d):
        k = lax.rem(row_hi + d, row_half)
        piece = (2 * k + 1 - row_lo) * share
        return remote(part(mirror, piece, share), a_in.at[d], a_send.at[d], a_recv.at[d], row_mate, c)

    def b_copy(d):
        there = lax.rem(row_hi + d, row_half) * 2 + row_lo
        return remote(a_sum.at[d], b_in.at[d - 1], b_send.at[d - 1], b_recv.at[d - 1], there, c)

    def y_copy(d):
        h = lax.rem(hi + d, half)
        return remote(part(plain, 2 * h + 1 - lo), y_in.at[d], y_send.at[d], y_recv.at[d], r, mate)

    def z_copy(d):
        there = lax.rem(hi + d, half) * 2 + lo
        return remote(y_sum.at[d], z_in.at[d - 1], z_send.at[d - 1], z_recv.at[d - 1], r, there)

    def m_copy(j):
        return remote(
            part(b_sum, j), m_in.at[turn], m_send.at[j], m_recv.at[turn], target, share * r + j
        )

    row_turns = list(range(1, row_half)) + [0]
    turns = list(range(1, half)) + [0]
    for d in row_turns:
        a_copy(d).start()
    for d in turns:
        y_copy(d).start()
    for d in row_turns:
        a_copy(d).wait_recv()
        piece = (2 * lax.rem(row_hi + d, row_half) + row_lo) * share
        a_sum[d] = mirror[pl.ds(piece * size, share * size)] + a_in[d]
        if d:
            b_copy(d).start()
    for d in turns[:-1]:
        y_copy(d).wait_recv()
        y_sum[d] = plain[pl.ds((2 * lax.rem(hi + d, half) + lo) * size, size)] + y_in[d]
        z_copy(d).start()
    for d in range(1, row_half):
        b_copy(d).wait_recv()
    total = a_sum[0]
    for d in range(1, row_half):
        total = total + b_in[d - 1]
    b_sum[...] = total
    for j in range(share):
        @pl.when(jnp.logical_not(is_self(j)))
        def _(j=j):
            m_copy(j).start()

        @pl.when(is_self(j))
        def _(j=j):
            m_in[turn] = b_sum[j * size:(j + 1) * size]
    y_copy(0).wait_recv()
    y_sum[0] = plain[pl.ds((2 * hi + lo) * size, size)] + y_in[0]
    for d in range(1, half):
        z_copy(d).wait_recv()
        y_sum[0] += z_in[d - 1]
    for i in range(share):
        @pl.when(jnp.logical_not((c // share == r) & (r + rows * i == c)))
        def _(i=i):
            remote(
                part(b_sum, 0), m_in.at[i], m_send.at[0], m_recv.at[i], r, mate
            ).wait_recv()
    for t in range(size):
        value = y_sum[0, t]
        for i in range(share):
            value = value + m_in[i, t]
        out[:, t * width:(t + 1) * width] = value

    for d in row_turns:
        a_copy(d).wait_send()
    for d in turns:
        y_copy(d).wait_send()
    for d in range(1, row_half):
        b_copy(d).wait_send()
    for d in range(1, half):
        z_copy(d).wait_send()
    for j in range(share):
        @pl.when(jnp.logical_not(is_self(j)))
        def _(j=j):
            m_copy(j).wait_send()


def reduce_products(plain, mirror, rows, cols):
    total, vec_count, width = plain.shape
    size = (total - 1) // cols
    share = cols // rows
    half, row_half = cols // 2, rows // 2
    dma = pltpu.SemaphoreType.DMA

    def room(*lead):
        return pltpu.VMEM((*lead, vec_count, width), jnp.float32)

    return pl.pallas_call(
        functools.partial(reduce_kernel, rows, cols, width),
        out_shape=jax.ShapeDtypeStruct((vec_count, size * width), jnp.float32),
        in_specs=[pl.BlockSpec(memory_space=pltpu.VMEM)] * 2,
        out_specs=pl.BlockSpec(memory_space=pltpu.VMEM),
        scratch_shapes=[
            room(half, size),
            room(half, size),
            room(half, size),
            room(row_half, share * size),
            room(row_half, share * size),
            room(row_half, share * size),
            room(share * size),
            room(share, size),
            dma((half,)), dma((half,)), dma((half,)), dma((half,)),
            dma((row_half,)), dma((row_half,)), dma((row_half,)), dma((row_half,)),
            dma((share,)), dma((share,)),
        ],
        compiler_params=pltpu.CompilerParams(
            collective_id=1, has_side_effects=True, vmem_limit_bytes=VMEM_BYTES
        ),
        name="reduce_products",
    )(plain, mirror)


def shards(vectors, tiles, tile_rows, tile_cols, tile_count):
    rows, cols = lax.axis_size("row"), lax.axis_size("col")
    off_diagonal = lax.axis_index("row") != lax.axis_index("col") % rows
    info = jnp.concatenate([tile_count, off_diagonal.astype(jnp.int32)[None]])
    own, mir = gather(vectors, rows, cols, tiles.shape[1])
    plain, mirror = apply_tiles(tile_rows, tile_cols, info, own, mir, tiles)
    return reduce_products(plain, mirror, rows, cols)


def solution(mesh):
    return jax.shard_map(
        shards,
        mesh=mesh,
        in_specs=(
            P(None, ("row", "col")),
            P(("row", "col"), None, None),
            P(("row", "col")),
            P(("row", "col")),
            P(("row", "col")),
        ),
        out_specs=P(None, ("row", "col")),
        check_vma=False,
    )
```

```python
import functools

import jax
import jax.numpy as jnp
from jax import lax
from jax.experimental import pallas as pl
from jax.experimental.pallas import tpu as pltpu
from jax.sharding import PartitionSpec as P

MESH = pl.DeviceIdType.MESH
VMEM_BYTES = 48 * 1024 * 1024


def remote(src, dst, send_sem, recv_sem, row, col):
    return pltpu.make_async_remote_copy(
        src_ref=src,
        dst_ref=dst,
        send_sem=send_sem,
        recv_sem=recv_sem,
        device_id=(row, col),
        device_id_type=MESH,
    )


def greet(row, col):
    pl.semaphore_signal(
        pltpu.get_barrier_semaphore(), inc=1, device_id=(row, col), device_id_type=MESH
    )


def order_table(lines, key, operand, places):
    slots = key.shape[1]
    keys = jnp.broadcast_to(key, (slots, slots))
    down = keys.T
    at = lax.broadcasted_iota(jnp.int32, (slots, slots), 0)
    along = lax.broadcasted_iota(jnp.int32, (slots, slots), 1)
    ahead = (down < keys) | ((down == keys) & (at < along))
    rank = jnp.sum(ahead.astype(jnp.int32), axis=0, keepdims=True)
    hit = jnp.broadcast_to(rank, (slots, slots)).T == along
    operands = jnp.broadcast_to(operand, (slots, slots)).T

    def pick(values):
        return jnp.sum(jnp.where(hit, values, 0), axis=0, keepdims=True)

    lines[0] = pick(at)
    lines[1] = pick(operands)
    lines[2] = pick(down)
    place = lax.broadcasted_iota(jnp.int32, (slots, slots), 1)
    for n in range(places // slots):
        spot = place + n * slots
        upto = jnp.sum((down <= spot).astype(jnp.int32), axis=0, keepdims=True)
        before = jnp.sum((down < spot).astype(jnp.int32), axis=0, keepdims=True)
        lines[3 + n] = jnp.where(upto > before, upto - 1, slots)


def kernel(
    rows, cols, width, group,
    x_hbm, tiles_hbm, rows_ref, cols_ref, count_ref, out,
    x_in, tiles, own, mir, lines, table, run_p, run_m, stage_p, stage_m,
    y_in, y_sum, z_in, a_in, a_sum, b_in, b_sum, m_in,
    local, line_send, mate_send, own_recv, mir_send, mir_recv,
    y_send, y_recv, z_send, z_recv, a_send, a_recv, b_send, b_recv, m_send, m_recv,
):
    r, c = lax.axis_index("row"), lax.axis_index("col")
    half, row_half = cols // 2, rows // 2
    hi, lo = c // 2, c % 2
    mate = c + 1 - 2 * lo
    row_lo, row_hi = r % 2, r // 2
    row_mate = r + 1 - 2 * row_lo
    share = cols // rows
    target = c % rows
    turn = c // rows
    size = y_in.shape[1]
    slots = tiles.shape[0]
    owns = target == r
    own_piece = (c // share == r) & owns

    def is_self(j):
        return owns & (share * r + j == c)

    x_copy = pltpu.make_async_copy(x_hbm, x_in, local.at[0])
    tiles_copy = pltpu.make_async_copy(tiles_hbm, tiles, local.at[1])
    x_copy.start()
    tiles_copy.start()

    greet(r, mate)
    for d in range(1, half):
        greet(r, lax.rem(hi + half - d, half) * 2 + lo)
    greet(row_mate, c)
    for d in range(1, row_half):
        greet(lax.rem(row_hi + row_half - d, row_half) * 2 + row_lo, c)
    for i in range(share):
        @pl.when(jnp.logical_not((c // share == r) & (r + rows * i == c)))
        def _(i=i):
            greet(c // share, r + rows * i)

    @pl.when(jnp.logical_not(owns))
    def _():
        greet(target, c)

    x_copy.wait()
    for t in range(size):
        own[c * size + t] = x_in[:, t * width:(t + 1) * width]
    receivers = half + row_half + share - jnp.where(own_piece, 1, 0) + jnp.where(owns, rows - 1, 0)
    pl.semaphore_wait(pltpu.get_barrier_semaphore(), receivers)

    def part(ref, index, count=1):
        return ref.at[pl.ds(index * size, count * size)]

    def to_line(d):
        there = lax.rem(hi + d, half) * 2 + lo
        return remote(part(own, c), part(own, c), line_send.at[d - 1], own_recv.at[c], r, there)

    def to_mate(index, n):
        return remote(part(own, index), part(own, index), mate_send.at[n], own_recv.at[index], r, mate)

    def mirror_sends(index, n):
        return [
            remote(
                part(own, index), part(mir, index), mir_send.at[n, d - 1], mir_recv.at[index],
                lax.rem(r + d, rows), c,
            )
            for d in range(1, rows)
        ]

    order = [c]
    for d in range(1, half):
        order.append(lax.rem(hi + half - d, half) * 2 + lo)
    order.append(mate)
    for d in range(1, half):
        order.append(lax.rem(hi + half - d, half) * 2 + 1 - lo)

    for d in range(1, half):
        to_line(d).start()
    to_mate(c, 0).start()

    @pl.when(owns)
    def _():
        for copy in mirror_sends(c, 0):
            copy.start()

    count = count_ref[0]
    live = lax.broadcasted_iota(jnp.int32, (1, slots), 1) < count
    row_line, col_line = rows_ref[...], cols_ref[...]
    never = own.shape[0]
    places = (lines.shape[0] // 2 - 3) * slots
    lines_m, lines_p = lines.at[0:lines.shape[0] // 2], lines.at[lines.shape[0] // 2:lines.shape[0]]
    both = live & (jnp.logical_not(owns) | (row_line != col_line))
    order_table(lines_m, jnp.where(both, col_line, never), row_line, places)
    order_table(lines_p, jnp.where(live, row_line, never), col_line, places)
    table_copy = pltpu.make_async_copy(lines, table, local.at[2])
    table_copy.start()
    run_p[slots] = jnp.zeros_like(run_p[slots])
    run_m[slots] = jnp.zeros_like(run_m[slots])

    for n in range(cols):
        index = order[n]
        if n:
            to_mate(index, 0).wait_recv()

            if n < half:
                to_mate(index, n).start()

        @pl.when(owns)
        def _(index=index, n=n):
            if n:
                for copy in mirror_sends(index, n):
                    copy.start()
            for t in range(size):
                mir[index * size + t] = own[index * size + t]

    table_copy.wait()
    tiles_copy.wait()

    def products(base, source, runs, contract):
        def body(g, carry):
            run, before = carry
            found = []
            for u in range(group):
                p = g * group + u
                slot = table[base, 0, p]
                found.append(
                    lax.dot_general(
                        source[table[base + 1, 0, p]], tiles[slot], (((1,), (contract,)), ((), ())),
                        preferred_element_type=jnp.float32,
                    )
                )
            for u in range(group):
                p = g * group + u
                key = table[base + 2, 0, p]
                run = jnp.where(key == before, run, 0.0) + found[u]
                runs[p] = run
                before = key
            return run, before

        start = (jnp.zeros((own.shape[1], width), jnp.float32), jnp.int32(-1))
        lax.fori_loop(0, slots // group, body, start)

    base_p = lines.shape[0] // 2

    def sum_at(base, runs, place):
        return runs[table[base + 3 + place // slots, 0, place % slots]]

    def mirror_at(place):
        return sum_at(0, run_m, place)

    def plain_at(place):
        return sum_at(base_p, run_p, place)

    def a_copy(d):
        return remote(stage_m.at[d], a_in.at[d], a_send.at[d], a_recv.at[d], row_mate, c)

    def b_copy(d):
        there = lax.rem(row_hi + d, row_half) * 2 + row_lo
        return remote(a_sum.at[d], b_in.at[d - 1], b_send.at[d - 1], b_recv.at[d - 1], there, c)

    def y_copy(d):
        return remote(stage_p.at[d], y_in.at[d], y_send.at[d], y_recv.at[d], r, mate)

    def z_copy(d):
        there = lax.rem(hi + d, half) * 2 + lo
        return remote(y_sum.at[d], z_in.at[d - 1], z_send.at[d - 1], z_recv.at[d - 1], r, there)

    def m_copy(j):
        return remote(
            part(b_sum, j), m_in.at[turn], m_send.at[j], m_recv.at[turn], target, share * r + j
        )

    row_turns = list(range(1, row_half)) + [0]
    turns = list(range(1, half)) + [0]

    products(0, own, run_m, 0)
    for d in row_turns:
        first = (2 * lax.rem(row_hi + d, row_half) + 1 - row_lo) * share * size
        for t in range(share * size):
            stage_m[d, t] = mirror_at(first + t)
        a_copy(d).start()

    @pl.when(jnp.logical_not(owns))
    def _():
        for n in range(cols):
            remote(
                part(own, order[n]), part(mir, order[n]), mir_send.at[n, 0], mir_recv.at[order[n]], row_mate, c
            ).wait_recv()

    products(base_p, mir, run_p, 1)
    for d in turns:
        first = (2 * lax.rem(hi + d, half) + 1 - lo) * size
        for t in range(size):
            stage_p[d, t] = plain_at(first + t)
        y_copy(d).start()
    for d in row_turns:
        a_copy(d).wait_recv()
        first = (2 * lax.rem(row_hi + d, row_half) + row_lo) * share * size
        for t in range(share * size):
            a_sum[d, t] = mirror_at(first + t) + a_in[d, t]
        if d:
            b_copy(d).start()
    for d in turns[:-1]:
        y_copy(d).wait_recv()
        first = (2 * lax.rem(hi + d, half) + lo) * size
        for t in range(size):
            y_sum[d, t] = plain_at(first + t) + y_in[d, t]
        z_copy(d).start()
    for d in range(1, row_half):
        b_copy(d).wait_recv()
    total = a_sum[0]
    for d in range(1, row_half):
        total = total + b_in[d - 1]
    b_sum[...] = total
    for j in range(share):
        @pl.when(jnp.logical_not(is_self(j)))
        def _(j=j):
            m_copy(j).start()

        @pl.when(is_self(j))
        def _(j=j):
            m_in[turn] = b_sum[j * size:(j + 1) * size]
    y_copy(0).wait_recv()
    for t in range(size):
        y_sum[0, t] = plain_at((2 * hi + lo) * size + t) + y_in[0, t]
    for d in range(1, half):
        z_copy(d).wait_recv()
        y_sum[0] += z_in[d - 1]
    for i in range(share):
        @pl.when(jnp.logical_not((c // share == r) & (r + rows * i == c)))
        def _(i=i):
            remote(
                part(b_sum, 0), m_in.at[i], m_send.at[0], m_recv.at[i], r, mate
            ).wait_recv()
    for t in range(size):
        value = y_sum[0, t]
        for i in range(share):
            value = value + m_in[i, t]
        out[:, t * width:(t + 1) * width] = value

    for d in range(1, half):
        to_line(d).wait_send()
    for n in range(half):
        to_mate(order[n], n).wait_send()

    @pl.when(owns)
    def _():
        for n in range(cols):
            for copy in mirror_sends(order[n], n):
                copy.wait_send()

    for d in row_turns:
        a_copy(d).wait_send()
    for d in turns:
        y_copy(d).wait_send()
    for d in range(1, row_half):
        b_copy(d).wait_send()
    for d in range(1, half):
        z_copy(d).wait_send()
    for j in range(share):
        @pl.when(jnp.logical_not(is_self(j)))
        def _(j=j):
            m_copy(j).wait_send()


def shards(vectors, tiles, tile_rows, tile_cols, tile_count):
    rows, cols = lax.axis_size("row"), lax.axis_size("col")
    slots, width = tiles.shape[0], tiles.shape[1]
    vec_count, length = vectors.shape
    size = length // width
    share = cols // rows
    half, row_half = cols // 2, rows // 2
    places = -(-(cols * size) // slots)
    dma = pltpu.SemaphoreType.DMA

    def room(*lead):
        return pltpu.VMEM((*lead, vec_count, width), jnp.float32)

    segment = pltpu.VMEM((cols * size, vec_count, width), vectors.dtype)
    on_vmem = pl.BlockSpec(memory_space=pltpu.VMEM)
    return pl.pallas_call(
        functools.partial(kernel, rows, cols, width, 8 if slots % 8 == 0 else 1),
        out_shape=jax.ShapeDtypeStruct((vec_count, length), jnp.float32),
        in_specs=[
            pl.BlockSpec(memory_space=pl.ANY),
            pl.BlockSpec(memory_space=pl.ANY),
            on_vmem,
            on_vmem,
            pl.BlockSpec(memory_space=pltpu.SMEM),
        ],
        out_specs=on_vmem,
        scratch_shapes=[
            pltpu.VMEM((vec_count, length), vectors.dtype),
            pltpu.VMEM(tiles.shape, tiles.dtype),
            segment,
            segment,
            pltpu.VMEM((2 * (3 + places), 1, slots), jnp.int32),
            pltpu.SMEM((2 * (3 + places), 1, slots), jnp.int32),
            room(slots + 1),
            room(slots + 1),
            room(half, size),
            room(row_half, share * size),
            room(half, size),
            room(half, size),
            room(half, size),
            room(row_half, share * size),
            room(row_half, share * size),
            room(row_half, share * size),
            room(share * size),
            room(share, size),
            dma((3,)), dma((half,)), dma((half,)), dma((cols,)), dma((cols, rows)), dma((cols,)),
            dma((half,)), dma((half,)), dma((half,)), dma((half,)),
            dma((row_half,)), dma((row_half,)), dma((row_half,)), dma((row_half,)),
            dma((share,)), dma((share,)),
        ],
        compiler_params=pltpu.CompilerParams(
            collective_id=0, has_side_effects=True, vmem_limit_bytes=VMEM_BYTES
        ),
        name="apply_symmetric",
    )(vectors, tiles, tile_rows.reshape(1, slots), tile_cols.reshape(1, slots), tile_count)


def solution(mesh):
    return jax.shard_map(
        shards,
        mesh=mesh,
        in_specs=(
            P(None, ("row", "col")),
            P(("row", "col"), None, None),
            P(("row", "col")),
            P(("row", "col")),
            P(("row", "col")),
        ),
        out_specs=P(None, ("row", "col")),
        check_vma=False,
    )
```

```python
import functools

import jax
import jax.numpy as jnp
from jax import lax
from jax.experimental import pallas as pl
from jax.experimental.pallas import tpu as pltpu
from jax.sharding import PartitionSpec as P

MESH = pl.DeviceIdType.MESH
VMEM_BYTES = 60 * 1024 * 1024


def remote(src, dst, send_sem, recv_sem, row, col):
    return pltpu.make_async_remote_copy(
        src_ref=src,
        dst_ref=dst,
        send_sem=send_sem,
        recv_sem=recv_sem,
        device_id=(row, col),
        device_id_type=MESH,
    )


def greet(row, col):
    pl.semaphore_signal(
        pltpu.get_barrier_semaphore(), inc=1, device_id=(row, col), device_id_type=MESH
    )


def order_table(lines, key, operand, places):
    slots = key.shape[1]
    keys = jnp.broadcast_to(key, (slots, slots))
    down = keys.T
    at = lax.broadcasted_iota(jnp.int32, (slots, slots), 0)
    along = lax.broadcasted_iota(jnp.int32, (slots, slots), 1)
    ahead = (down < keys) | ((down == keys) & (at < along))
    rank = jnp.sum(ahead.astype(jnp.int32), axis=0, keepdims=True)
    hit = jnp.broadcast_to(rank, (slots, slots)).T == along
    operands = jnp.broadcast_to(operand, (slots, slots)).T

    def pick(values):
        return jnp.sum(jnp.where(hit, values, 0), axis=0, keepdims=True)

    lines[0] = pick(at)
    lines[1] = pick(operands)
    lines[2] = pick(down)
    place = lax.broadcasted_iota(jnp.int32, (slots, slots), 1)
    for n in range(places // slots):
        spot = place + n * slots
        upto = jnp.sum((down <= spot).astype(jnp.int32), axis=0, keepdims=True)
        before = jnp.sum((down < spot).astype(jnp.int32), axis=0, keepdims=True)
        lines[3 + n] = jnp.where(upto > before, upto - 1, slots)


def kernel(
    rows, cols, width, group,
    x_hbm, tiles_hbm, rows_hbm, cols_hbm, count_ref, out,
    x_in, tiles, rows_ref, cols_ref, own, mir, lines_m, lines_p, table_m, table_p, run_p, run_m, stage_p, stage_m,
    y_in, y_sum, z_in, a_in, a_sum, b_in, b_sum, m_in,
    local, line_send, mate_send, own_recv, mir_send, mir_recv,
    y_send, y_recv, z_send, z_recv, a_send, a_recv, b_send, b_recv, m_send, m_recv,
):
    r, c = lax.axis_index("row"), lax.axis_index("col")
    half, row_half = cols // 2, rows // 2
    hi, lo = c // 2, c % 2
    mate = c + 1 - 2 * lo
    row_lo, row_hi = r % 2, r // 2
    row_mate = r + 1 - 2 * row_lo
    share = cols // rows
    target = c % rows
    turn = c // rows
    size = y_in.shape[1]
    slots = tiles.shape[0]
    owns = target == r
    own_piece = (c // share == r) & owns

    def is_self(j):
        return owns & (share * r + j == c)

    x_copy = pltpu.make_async_copy(x_hbm, x_in, local.at[0])
    tiles_copy = pltpu.make_async_copy(tiles_hbm, tiles, local.at[1])
    rows_copy = pltpu.make_async_copy(rows_hbm, rows_ref, local.at[2])
    cols_copy = pltpu.make_async_copy(cols_hbm, cols_ref, local.at[3])
    x_copy.start()
    rows_copy.start()
    cols_copy.start()

    greet(r, mate)
    for d in range(1, half):
        greet(r, lax.rem(hi + half - d, half) * 2 + lo)
    greet(row_mate, c)
    for d in range(1, row_half):
        greet(lax.rem(row_hi + row_half - d, row_half) * 2 + row_lo, c)
    for i in range(share):
        @pl.when(jnp.logical_not((c // share == r) & (r + rows * i == c)))
        def _(i=i):
            greet(c // share, r + rows * i)

    @pl.when(jnp.logical_not(owns))
    def _():
        greet(target, c)

    x_copy.wait()
    for t in range(size):
        own[c * size + t] = x_in[:, t * width:(t + 1) * width]
    tiles_copy.start()
    receivers = half + row_half + share - jnp.where(own_piece, 1, 0) + jnp.where(owns, rows - 1, 0)
    pl.semaphore_wait(pltpu.get_barrier_semaphore(), receivers)

    def part(ref, index, count=1):
        return ref.at[pl.ds(index * size, count * size)]

    def to_line(d):
        there = lax.rem(hi + d, half) * 2 + lo
        return remote(part(own, c), part(own, c), line_send.at[d - 1], own_recv.at[c], r, there)

    def to_mate(index, n):
        return remote(part(own, index), part(own, index), mate_send.at[n], own_recv.at[index], r, mate)

    def mirror_sends(index, n):
        return [
            remote(
                part(own, index), part(mir, index), mir_send.at[n, d - 1], mir_recv.at[index],
                lax.rem(r + d, rows), c,
            )
            for d in range(1, rows)
        ]

    order = [c]
    for d in range(1, half):
        order.append(lax.rem(hi + half - d, half) * 2 + lo)
    order.append(mate)
    for d in range(1, half):
        order.append(lax.rem(hi + half - d, half) * 2 + 1 - lo)

    for d in range(1, half):
        to_line(d).start()
    to_mate(c, 0).start()

    @pl.when(owns)
    def _():
        for copy in mirror_sends(c, 0):
            copy.start()

    rows_copy.wait()
    cols_copy.wait()
    live = lax.broadcasted_iota(jnp.int32, (1, slots), 1) < count_ref[0]
    never = own.shape[0]
    places = (lines_m.shape[0] - 3) * slots
    both = live & (jnp.logical_not(owns) | (rows_ref[...] != cols_ref[...]))
    order_table(lines_m, jnp.where(both, cols_ref[...], never), rows_ref[...], places)
    table_m_copy = pltpu.make_async_copy(lines_m, table_m, local.at[4])
    table_m_copy.start()
    run_p[slots] = jnp.zeros_like(run_p[slots])
    run_m[slots] = jnp.zeros_like(run_m[slots])

    for n in range(cols):
        index = order[n]
        if n:
            to_mate(index, 0).wait_recv()

            if n < half:
                to_mate(index, n).start()

        @pl.when(owns)
        def _(index=index, n=n):
            if n:
                for copy in mirror_sends(index, n):
                    copy.start()
            for t in range(size):
                mir[index * size + t] = own[index * size + t]

    table_m_copy.wait()
    tiles_copy.wait()

    def products(table, source, runs, contract):
        def body(g, carry):
            run, before = carry
            found = []
            for u in range(group):
                p = g * group + u
                slot = table[0, 0, p]
                found.append(
                    lax.dot_general(
                        source[table[1, 0, p]], tiles[slot], (((1,), (contract,)), ((), ())),
                        preferred_element_type=jnp.float32,
                    )
                )
            for u in range(group):
                p = g * group + u
                key = table[2, 0, p]
                run = jnp.where(key == before, run, 0.0) + found[u]
                runs[p] = run
                before = key
            return run, before

        start = (jnp.zeros((own.shape[1], width), jnp.float32), jnp.int32(-1))
        lax.fori_loop(0, slots // group, body, start)

    def sum_at(table, runs, place):
        return runs[table[3 + place // slots, 0, place % slots]]

    def mirror_at(place):
        return sum_at(table_m, run_m, place)

    def plain_at(place):
        return sum_at(table_p, run_p, place)

    def a_copy(d):
        return remote(stage_m.at[d], a_in.at[d], a_send.at[d], a_recv.at[d], row_mate, c)

    def b_copy(d):
        there = lax.rem(row_hi + d, row_half) * 2 + row_lo
        return remote(a_sum.at[d], b_in.at[d - 1], b_send.at[d - 1], b_recv.at[d - 1], there, c)

    def y_copy(d):
        return remote(stage_p.at[d], y_in.at[d], y_send.at[d], y_recv.at[d], r, mate)

    def z_copy(d):
        there = lax.rem(hi + d, half) * 2 + lo
        return remote(y_sum.at[d], z_in.at[d - 1], z_send.at[d - 1], z_recv.at[d - 1], r, there)

    def m_copy(j):
        return remote(
            part(b_sum, j), m_in.at[turn], m_send.at[j], m_recv.at[turn], target, share * r + j
        )

    row_turns = list(range(1, row_half)) + [0]
    turns = list(range(1, half)) + [0]

    products(table_m, own, run_m, 0)
    for d in row_turns:
        first = (2 * lax.rem(row_hi + d, row_half) + 1 - row_lo) * share * size
        for t in range(share * size):
            stage_m[d, t] = mirror_at(first + t)
        a_copy(d).start()
    order_table(lines_p, jnp.where(live, rows_ref[...], never), cols_ref[...], places)
    table_p_copy = pltpu.make_async_copy(lines_p, table_p, local.at[5])
    table_p_copy.start()
    for d in row_turns:
        a_copy(d).wait_recv()
        first = (2 * lax.rem(row_hi + d, row_half) + row_lo) * share * size
        for t in range(share * size):
            a_sum[d, t] = mirror_at(first + t) + a_in[d, t]
        if d:
            b_copy(d).start()
    table_p_copy.wait()

    @pl.when(jnp.logical_not(owns))
    def _():
        for n in range(cols):
            remote(
                part(own, order[n]), part(mir, order[n]), mir_send.at[n, 0], mir_recv.at[order[n]], row_mate, c
            ).wait_recv()

    products(table_p, mir, run_p, 1)
    for d in turns:
        first = (2 * lax.rem(hi + d, half) + 1 - lo) * size
        for t in range(size):
            stage_p[d, t] = plain_at(first + t)
        y_copy(d).start()
    for d in range(1, row_half):
        b_copy(d).wait_recv()
    total = a_sum[0]
    for d in range(1, row_half):
        total = total + b_in[d - 1]
    b_sum[...] = total
    for j in range(share):
        @pl.when(jnp.logical_not(is_self(j)))
        def _(j=j):
            m_copy(j).start()

        @pl.when(is_self(j))
        def _(j=j):
            m_in[turn] = b_sum[j * size:(j + 1) * size]
    for d in turns[:-1]:
        y_copy(d).wait_recv()
        first = (2 * lax.rem(hi + d, half) + lo) * size
        for t in range(size):
            y_sum[d, t] = plain_at(first + t) + y_in[d, t]
        z_copy(d).start()
    y_copy(0).wait_recv()
    for t in range(size):
        y_sum[0, t] = plain_at((2 * hi + lo) * size + t) + y_in[0, t]
    for d in range(1, half):
        z_copy(d).wait_recv()
        y_sum[0] += z_in[d - 1]
    for i in range(share):
        @pl.when(jnp.logical_not((c // share == r) & (r + rows * i == c)))
        def _(i=i):
            remote(
                part(b_sum, 0), m_in.at[i], m_send.at[0], m_recv.at[i], r, mate
            ).wait_recv()
    for t in range(size):
        value = y_sum[0, t]
        for i in range(share):
            value = value + m_in[i, t]
        out[:, t * width:(t + 1) * width] = value

    for d in range(1, half):
        to_line(d).wait_send()
    for n in range(half):
        to_mate(order[n], n).wait_send()

    @pl.when(owns)
    def _():
        for n in range(cols):
            for copy in mirror_sends(order[n], n):
                copy.wait_send()

    for d in row_turns:
        a_copy(d).wait_send()
    for d in turns:
        y_copy(d).wait_send()
    for d in range(1, row_half):
        b_copy(d).wait_send()
    for d in range(1, half):
        z_copy(d).wait_send()
    for j in range(share):
        @pl.when(jnp.logical_not(is_self(j)))
        def _(j=j):
            m_copy(j).wait_send()


def shards(vectors, tiles, tile_rows, tile_cols, tile_count):
    rows, cols = lax.axis_size("row"), lax.axis_size("col")
    slots, width = tiles.shape[0], tiles.shape[1]
    vec_count, length = vectors.shape
    size = length // width
    share = cols // rows
    half, row_half = cols // 2, rows // 2
    places = -(-(cols * size) // slots)
    dma = pltpu.SemaphoreType.DMA

    def room(*lead):
        return pltpu.VMEM((*lead, vec_count, width), jnp.float32)

    segment = pltpu.VMEM((cols * size, vec_count, width), vectors.dtype)
    on_vmem = pl.BlockSpec(memory_space=pltpu.VMEM)
    in_hbm = pl.BlockSpec(memory_space=pltpu.HBM)
    return pl.pallas_call(
        functools.partial(kernel, rows, cols, width, 8 if slots % 8 == 0 else 1),
        out_shape=jax.ShapeDtypeStruct((vec_count, length), jnp.float32),
        in_specs=[
            in_hbm,
            in_hbm,
            in_hbm,
            in_hbm,
            pl.BlockSpec(memory_space=pltpu.SMEM),
        ],
        out_specs=on_vmem,
        scratch_shapes=[
            pltpu.VMEM((vec_count, length), vectors.dtype),
            pltpu.VMEM(tiles.shape, tiles.dtype),
            pltpu.VMEM((1, slots), jnp.int32),
            pltpu.VMEM((1, slots), jnp.int32),
            segment,
            segment,
            pltpu.VMEM((3 + places, 1, slots), jnp.int32),
            pltpu.VMEM((3 + places, 1, slots), jnp.int32),
            pltpu.SMEM((3 + places, 1, slots), jnp.int32),
            pltpu.SMEM((3 + places, 1, slots), jnp.int32),
            room(slots + 1),
            room(slots + 1),
            room(half, size),
            room(row_half, share * size),
            room(half, size),
            room(half, size),
            room(half, size),
            room(row_half, share * size),
            room(row_half, share * size),
            room(row_half, share * size),
            room(share * size),
            room(share, size),
            dma((6,)), dma((half,)), dma((half,)), dma((cols,)), dma((cols, rows)), dma((cols,)),
            dma((half,)), dma((half,)), dma((half,)), dma((half,)),
            dma((row_half,)), dma((row_half,)), dma((row_half,)), dma((row_half,)),
            dma((share,)), dma((share,)),
        ],
        compiler_params=pltpu.CompilerParams(
            collective_id=0, has_side_effects=True, vmem_limit_bytes=VMEM_BYTES
        ),
        name="apply_symmetric",
    )(vectors, tiles, tile_rows.reshape(1, slots), tile_cols.reshape(1, slots), tile_count)


def solution(mesh):
    return jax.shard_map(
        shards,
        mesh=mesh,
        in_specs=(
            P(None, ("row", "col")),
            P(("row", "col"), None, None),
            P(("row", "col")),
            P(("row", "col")),
            P(("row", "col")),
        ),
        out_specs=P(None, ("row", "col")),
        check_vma=False,
    )
```
